256 devices in a mesh: row: 64 (over y, z, core), col: 4 (over x).
Axes of the slice: x: 4, y: 4, z: 8, core: 2. Of those that a mesh axis runs over, the one named last changes fastest.
Arguments:
- grad_out: bfloat16 [524288, 512], P('row', 'col'), may hold values from -6 to 6
- features: bfloat16 [524288, 512], P('row', 'col')
- weight: bfloat16 [512, 512], P(None, 'col'), may hold values from -0.25 to 0.25
- tiles: bfloat16 [12288, 128, 128], P('row'), may hold values from -0.75 to 0.75
- tile_row_block: int32 [12288], P('row'), may hold values from 0 to 63
- tile_owner: int32 [12288, 1], P('row'), may hold values from 0 to 63; in each aligned block of 192 rows (0 to 191, 192 to 383, ...) at most 4 rows name the same one
- tile_local: int32 [12288], P('row'), may hold values from 0 to 63
- degrees: int32 [524288], P('row'), may hold values from 1 to 8
- live: int32 [64], P('row'), may hold values from 1 to 192, 9216 in all
Outputs:
- grad_pre: bfloat16 [524288, 512], P('row', 'col')
- grad_weight: float32 [512, 512], P(None, 'col')
The draws below stay inside these ranges and needn't reach their ends.
Inputs may be any that keep to these rules, and one draw needn't show every extreme that they name: `tile_owner`: within the 192 tile slots of one index of row, no owner is named more than 4 times, and 4 is reached in some index of row. Some index of row has all 192 slots live.
All inputs are finite; a program needn't handle non-finite values. No bound on the sum of `live` on one device may be relied on, other than what follows from the above.
Results may differ from the reference program's by a relative error of at most 0.0061.
Values may be sent and summed in bfloat16 or wider, within the bound.
No kernel may reach another device: no remote copies, remote signals or barrier semaphores. Data moves between devices by JAX's collectives and lax.ppermute only.
A program may use at most 128 MiB of HBM per device.

```python
import math
import jax
import jax.numpy as jnp
import numpy as np
from jax import lax

F = 512
TILE = 128
BLOCKS_PER_ROW = 64
TILES_DEV = 192
CAP = 4
NODES = 524288
TOTAL_TILE_SLOTS = 12288
N_ROW = 64


def draw_features(key, part):
    key = jax.random.fold_in(key, 11)
    values = jax.random.normal(key, (NODES, F), jnp.float32)
    return jnp.maximum(values, 0.0).astype(jnp.bfloat16)


def plant(array, stream_key, least, top_value):
    dims = array.shape
    place = [jax.random.randint(jax.random.fold_in(stream_key, axis), (), 0, dims[axis]) for axis in range(len(dims))]
    array = array.at[tuple(place)].set(least)
    longest = dims.index(max(dims))
    place[longest] = (place[longest] + 1) % dims[longest]
    return array.at[tuple(place)].set(top_value)


def steps_of(own_key, shape, shards, smallest, top_value):
    loudness, own = 1.0, jax.random.fold_in(own_key, 6)
    for axis_at, shards_of in shards:
        steps = jnp.exp(jax.random.uniform(jax.random.fold_in(own, axis_at), (shards_of,), jnp.float32, smallest / len(shards), top_value / len(shards)))
        loudness = loudness * jnp.repeat(steps, shape[axis_at] // shards_of).reshape([-1 if axis == axis_at else 1 for axis in range(len(shape))])
    return loudness


def split_up(amount, total, limit, skew):
    weights = [(1 << 20) // math.isqrt(grade ** skew) + 1 for grade in range(2, amount + 1)]
    spare, given = total - limit - (amount - 1), [1] * (amount - 1)
    while spare > 0:
        free = [i for i in range(amount - 1) if given[i] < limit]
        mass, budget = sum([weights[i] for i in free]), spare
        for i in free:
            addition = min(limit - given[i], max(1, budget * weights[i] // mass), spare)
            given[i] = given[i] + addition
            spare = spare - addition
    return np.array([limit] + given)


def ragged_sizes(stream_key, count, total, limit, lean):
    if count == 2:
        one = jax.random.randint(stream_key, (), max(1, total - limit), min(limit, total - 1) + 1)
        return jnp.stack([one, total - one])
    sizes = jnp.asarray(split_up(count, total, limit, lean), jnp.int32)
    twos = (count - 1) // 2
    giver, taker = sizes[1:1 + 2 * twos:2], sizes[2:2 + 2 * twos:2]
    slack = jnp.minimum(giver - 1, limit - taker)
    shifted = jax.random.randint(jax.random.fold_in(stream_key, 1), (twos,), 0, 1 << 20) % (slack + 1)
    sizes = sizes.at[1:1 + 2 * twos:2].set(giver - shifted).at[2:2 + 2 * twos:2].set(taker + shifted)
    return sizes[jax.random.permutation(jax.random.fold_in(stream_key, 2), count)]


def shared_out(stream_key, own, number, rows, number_of, top, limit, slope):
    sequence = jax.random.permutation(stream_key, number_of)
    heavy_load, common = portions_of(number_of, rows * top, limit, slope, True), portions_of(number_of, rows * top, limit, slope, False)
    places = jnp.arange(number_of)

    def named(sizes, rotation):
        used = int((sizes > 0).sum())
        fixed = max(1, used // 4)
        shifted = fixed + (places - fixed + rotation * (used - fixed)) % max(1, number_of - fixed)
        return jnp.zeros((number_of,), jnp.int32).at[sequence[jnp.where(places < fixed, places, shifted)]].set(jnp.asarray(sizes, jnp.int32))

    sizes = jnp.where(number % 4 == 0, named(heavy_load, number // 4), named(common, number - number // 4 - 1))
    mixed = jax.random.permutation(jax.random.fold_in(own, 3), number_of)
    giver, receiver = mixed[0:number_of // 2 * 2:2], mixed[1:number_of // 2 * 2:2]
    slack = jnp.minimum(sizes[giver] - 1, limit - sizes[receiver]) // 2
    slack = jnp.where((giver == sequence[0]) | (receiver == sequence[0]) | (sizes[receiver] == 0), 0, jnp.maximum(slack, 0))
    shifted = jax.random.randint(jax.random.fold_in(own, 4), (number_of // 2,), 0, 1 << 20) % (slack + 1)
    sizes = sizes.at[giver].add(-shifted).at[receiver].add(shifted)
    items = jnp.searchsorted(jnp.cumsum(sizes), jnp.arange(rows * top), side="right").astype(jnp.int32)
    table = items.reshape(top, rows).T
    table = table[jax.random.permutation(jax.random.fold_in(own, 1), rows)]
    rotation = jax.random.randint(jax.random.fold_in(own, 2), (rows, 1), 0, top)
    return jnp.take_along_axis(table, (jnp.arange(top)[None, :] + rotation) % top, axis=1)


def portions_of(amount, total, most, lean, full):
    portions = [(1 << 20) // math.isqrt(grade ** lean) + 1 for grade in range(1, amount + 1)]
    largest = most if full else min(most, max(-(-total // amount), total * portions[0] // sum(portions)))
    least = 1 if total - largest >= amount - 1 else 0
    counts, surplus = [largest] + [least] * (amount - 1), total - largest - least * (amount - 1)
    while surplus > 0:
        movable = [i for i in range(1, amount) if counts[i] < largest] or [i for i in range(1, amount) if counts[i] < most]
        pool, remaining = sum([portions[i] for i in movable]), surplus
        for i in movable:
            addition = min(most - counts[i], max(1, remaining * portions[i] // pool), surplus)
            counts[i] = counts[i] + addition
            surplus = surplus - addition
    return np.array(counts)


def centred(key, dims, deviation, most, split=(), held_as=jnp.bfloat16):
    factor_of = steps_of(key, dims, split, -0.22, 0.18) if split else 1.0
    drawn = jax.random.normal(key, dims, jnp.float32) * deviation * factor_of
    return jnp.minimum(jnp.maximum(drawn, -most), most).astype(held_as)


def setup_inputs(seed: int = 0) -> dict:
    seeds = jax.random.split(jax.random.key(seed), 10)
    grad_out = centred(seeds[0], (NODES, F), 1.0, 6.0, ((0, 64), (1, 4)))
    features = draw_features(jax.random.fold_in(seeds[9], 71), 0)
    weight = centred(seeds[2], (F, F), F ** -0.5, 0.25, ((1, 4),))
    tiles = centred(seeds[3], (TOTAL_TILE_SLOTS, TILE, TILE), 64 ** -0.5, 0.75, ((0, 64),))
    tile_row_block = plant(jax.random.randint(seeds[4], (TOTAL_TILE_SLOTS,), 0, BLOCKS_PER_ROW), jax.random.fold_in(seeds[4], 1), 0, BLOCKS_PER_ROW - 1).astype(jnp.int32)
    tile_owner_keys = jax.random.split(jax.random.fold_in(seeds[5], 1), TOTAL_TILE_SLOTS // TILES_DEV)
    tile_owner_turns = jax.random.permutation(jax.random.fold_in(seeds[5], 3), TOTAL_TILE_SLOTS // TILES_DEV)
    tile_owner = jax.vmap(lambda own, number: shared_out(jax.random.fold_in(seeds[5], 2), own, number, TILES_DEV, N_ROW, 1, CAP, 2))(tile_owner_keys, tile_owner_turns).reshape((TOTAL_TILE_SLOTS, 1))
    tile_local = plant(jax.random.randint(seeds[6], (TOTAL_TILE_SLOTS,), 0, BLOCKS_PER_ROW), jax.random.fold_in(seeds[6], 1), 0, BLOCKS_PER_ROW - 1).astype(jnp.int32)
    degrees = plant(jax.random.randint(seeds[7], (NODES,), 1, 9), jax.random.fold_in(seeds[7], 1), 1, 8).astype(jnp.int32)
    live = ragged_sizes(seeds[8], N_ROW, (N_ROW * TILES_DEV * 3) // 4, TILES_DEV, 2).astype(jnp.int32)
    return {"grad_out": grad_out, "features": features, "weight": weight, "tiles": tiles, "tile_row_block": tile_row_block, "tile_owner": tile_owner, "tile_local": tile_local, "degrees": degrees, "live": live}


def reference(grad_out, features, weight, tiles, tile_row_block, tile_owner, tile_local, degrees, live):
    scale = lax.rsqrt(degrees.astype(jnp.float32))
    scaled = (grad_out.astype(jnp.float32) * scale[:, None]).astype(jnp.bfloat16)
    scaled_blocks = scaled.reshape(N_ROW * BLOCKS_PER_ROW, TILE, F)
    owning_indices = tile_owner[:, 0]

    def one_device(total, index):
        first = (index * TILES_DEV).astype(jnp.int32)
        tile_blocks = lax.dynamic_slice_in_dim(tiles, first, TILES_DEV, 0)
        rows = lax.dynamic_slice_in_dim(tile_row_block, first, TILES_DEV, 0)
        owner = lax.dynamic_slice_in_dim(owning_indices, first, TILES_DEV, 0)
        local = lax.dynamic_slice_in_dim(tile_local, first, TILES_DEV, 0)
        source_features = scaled_blocks[index * BLOCKS_PER_ROW + rows]
        tile_product = jnp.einsum('buv,buz->bvz', tile_blocks.astype(jnp.float32), source_features.astype(jnp.float32)).astype(jnp.bfloat16)
        alive = jnp.arange(TILES_DEV) < live[index]
        tile_product = jnp.where(alive[:, None, None], tile_product.astype(jnp.float32), 0.0)
        target = owner * BLOCKS_PER_ROW + local
        return (total.at[target].add(tile_product), None)
    start = jnp.zeros((N_ROW * BLOCKS_PER_ROW, TILE, F), jnp.float32)
    summed_partials, unused = lax.scan(one_device, start, jnp.arange(N_ROW, dtype=jnp.int32))
    summed_partials = summed_partials.reshape(NODES, F)
    propagated = (summed_partials * scale[:, None]).astype(jnp.bfloat16)
    back = jnp.dot(propagated, weight.T, preferred_element_type=jnp.float32)
    grad_pre = jnp.where(features > 0, back, 0.0).astype(jnp.bfloat16)
    grad_weight = jnp.dot(features.T, propagated, preferred_element_type=jnp.float32) / math.sqrt(NODES)
    return (grad_pre, grad_weight)
```

```python
import functools
import math

import jax
import jax.numpy as jnp
from jax import lax
from jax.experimental import pallas as pl
from jax.experimental.pallas import tpu as pltpu
from jax.sharding import PartitionSpec as P

PLACES = 4
LABEL_ROWS = 16
SPLIT = (64, 64)
VMEM = 48 * 1024 * 1024


def product_kernel(
    row_block, owner, local, live, tiles, scaled, out, count, labels, *, first, rows, group, label
):
    step = pl.program_id(0)
    size = tiles.shape[1]

    @pl.when(step == 0)
    def _():
        def clear(i, carry):
            count[i] = 0
            return carry

        lax.fori_loop(0, out.shape[0], clear, 0)
        if label:
            labels[...] = jnp.full(labels.shape, -1.0, labels.dtype)

    lane = lax.broadcasted_iota(jnp.int32, (LABEL_ROWS, size), 1)
    for i in range(group):
        tile = step * group + i
        peer = owner[tile]
        place = count[peer]
        count[peer] = place + 1
        source = scaled[pl.ds(pl.multiple_of(row_block[tile] * size, size), size), :]
        product = lax.dot_general(
            tiles[i, :, first : first + rows],
            source,
            (((0,), (0,)), ((), ())),
            preferred_element_type=jnp.float32,
        )
        out[peer, pl.ds(pl.multiple_of(place * rows, rows), rows), :] = product.astype(out.dtype)
        if label:
            value = jnp.where(tile < live[0], local[tile], -1).astype(jnp.float32)
            old = labels[peer].astype(jnp.float32)
            labels[peer] = jnp.where(lane == place, value, old).astype(labels.dtype)

    if label:

        @pl.when(step == pl.num_programs(0) - 1)
        def _():
            out[:, PLACES * rows :, :] = labels[...]


def products(row_block, owner, local, live, tiles, scaled, peers, first, rows, label):
    tile_count, size, _ = tiles.shape
    width = scaled.shape[1]
    group = 16
    extra = LABEL_ROWS if label else 0
    return pl.pallas_call(
        functools.partial(product_kernel, first=first, rows=rows, group=group, label=label),
        grid_spec=pltpu.PrefetchScalarGridSpec(
            num_scalar_prefetch=4,
            grid=(tile_count // group,),
            in_specs=[
                pl.BlockSpec((group, size, size), lambda i, *_: (i, 0, 0)),
                pl.BlockSpec(scaled.shape, lambda i, *_: (0, 0)),
            ],
            out_specs=pl.BlockSpec((peers, PLACES * rows + extra, width), lambda i, *_: (0, 0, 0)),
            scratch_shapes=[
                pltpu.SMEM((peers,), jnp.int32),
                pltpu.VMEM((peers, LABEL_ROWS, width), jnp.bfloat16),
            ],
        ),
        out_shape=jax.ShapeDtypeStruct((peers, PLACES * rows + extra, width), jnp.bfloat16),
        compiler_params=pltpu.CompilerParams(vmem_limit_bytes=VMEM),
        cost_estimate=pl.CostEstimate(
            flops=2 * tile_count * size * rows * width,
            bytes_accessed=2 * tiles.size + 2 * scaled.size + 2 * peers * PLACES * rows * width,
            transcendentals=0,
        ),
        name="products",
    )(row_block, owner, local, live, tiles, scaled)


def sum_kernel(labels, incoming, scale, low, high, total, *, rows, group):
    step = pl.program_id(0)
    half = low.shape[0]

    @pl.when(step == 0)
    def _():
        total[...] = jnp.zeros_like(total)

    for i in range(group):
        for place in range(PLACES):
            block = labels[(step * group + i) * PLACES + place]
            total[block] += incoming[i, place * rows : (place + 1) * rows, :].astype(jnp.float32)

    @pl.when(step == pl.num_programs(0) - 1)
    def _():
        low[...] = (total[:half] * scale[:half]).astype(low.dtype)
        high[...] = (total[half : 2 * half] * scale[half:]).astype(high.dtype)


def sums(labels, incoming, scale, rows):
    peers, depth, width = incoming.shape
    blocks = scale.shape[0]
    group = 8
    return pl.pallas_call(
        functools.partial(sum_kernel, rows=rows, group=group),
        grid_spec=pltpu.PrefetchScalarGridSpec(
            num_scalar_prefetch=1,
            grid=(peers // group,),
            in_specs=[
                pl.BlockSpec((group, depth, width), lambda i, *_: (i, 0, 0)),
                pl.BlockSpec(scale.shape, lambda i, *_: (0, 0, 0)),
            ],
            out_specs=[pl.BlockSpec((blocks // 2, rows, width), lambda i, *_: (0, 0, 0))] * 2,
            scratch_shapes=[pltpu.VMEM((blocks + 1, rows, width), jnp.float32)],
        ),
        out_shape=[jax.ShapeDtypeStruct((blocks // 2, rows, width), jnp.bfloat16)] * 2,
        compiler_params=pltpu.CompilerParams(vmem_limit_bytes=VMEM),
        cost_estimate=pl.CostEstimate(
            flops=incoming.size,
            bytes_accessed=2 * incoming.size + 4 * scale.size + 2 * scale.size,
            transcendentals=0,
        ),
        name="sums",
    )(labels, incoming, scale)


def back_kernel(*refs, half):
    low, high, (weight, features), out = refs[:4], refs[4:8], refs[8:10], refs[-1]
    rows, width = features.shape[1:]
    nodes = features.shape[0] * rows

    def run(parts):
        whole = jnp.concatenate([part[...].reshape(nodes, width) for part in parts], axis=1)
        back = lax.dot_general(
            whole, weight[...], (((1,), (0,)), ((), ())), preferred_element_type=jnp.float32
        ).reshape(features.shape)
        mask = features[...].astype(jnp.float32) > 0
        out[...] = jnp.where(mask, back, 0.0).astype(out.dtype)

    @pl.when(pl.program_id(0) < half)
    def _():
        run(low)

    @pl.when(pl.program_id(0) >= half)
    def _():
        run(high)


def back(low, high, weight, features, before, first, rows):
    blocks, size, width = features.shape
    steps = 4
    group = blocks // steps
    half = steps // 2
    spot = first // rows
    piece = pl.BlockSpec((group, rows, width), lambda i: (i, spot, 0))
    specs = [pl.BlockSpec((group, rows, width), lambda i: (jnp.minimum(i, half - 1), 0, 0))] * 4
    specs += [pl.BlockSpec((group, rows, width), lambda i: (jnp.maximum(i - half, 0), 0, 0))] * 4
    specs += [pl.BlockSpec(weight.shape, lambda i: (0, 0)), piece]
    args = [*low, *high, weight, features]
    aliases = {}
    if before is not None:
        specs.append(pl.BlockSpec(memory_space=pl.ANY))
        args.append(before)
        aliases = {len(args) - 1: 0}
    return pl.pallas_call(
        functools.partial(back_kernel, half=half),
        grid=(steps,),
        in_specs=specs,
        out_specs=piece,
        out_shape=jax.ShapeDtypeStruct(features.shape, jnp.bfloat16),
        input_output_aliases=aliases,
        compiler_params=pltpu.CompilerParams(vmem_limit_bytes=VMEM),
        cost_estimate=pl.CostEstimate(
            flops=2 * blocks * rows * width * weight.shape[0],
            bytes_accessed=2 * blocks * rows * (weight.shape[0] + 2 * width),
            transcendentals=0,
        ),
        name="back",
    )(*args)


def ring(shift, size):
    return [(i, (i + shift) % size) for i in range(size)]


def exchange(block):
    return lax.all_to_all(block, "row", split_axis=0, concat_axis=0, tiled=True)


def col_gather(low, high):
    size = lax.axis_size("col")
    ahead, behind = ring(1, size), ring(-1, size)
    low_left = lax.ppermute(low, "col", ahead)
    high_right = lax.ppermute(high, "col", behind)
    high_left = lax.ppermute(high, "col", ahead)
    low_right = lax.ppermute(low, "col", behind)
    low_far = lax.ppermute(low_left, "col", ahead)
    high_far = lax.ppermute(high_right, "col", behind)
    return (low, low_left, low_far, low_right), (high, high_left, high_far, high_right)


def weight_rows(weight):
    size = lax.axis_size("col")
    width = weight.shape[1]
    me = lax.axis_index("col")
    parts = []
    for shift in range(size):
        start = lax.rem(me + shift, size) * width
        slab = lax.dynamic_slice_in_dim(weight, start, width, 0)
        parts.append(slab if shift == 0 else lax.ppermute(slab, "col", ring(shift, size)))
    return jnp.concatenate(parts, axis=1).T


def per_device(
    grad_out, features, weight, tiles, tile_row_block, tile_owner, tile_local, degrees, live
):
    node_rows, width = grad_out.shape
    size = tiles.shape[1]
    blocks = node_rows // size
    peers = lax.axis_size("row")
    cols = lax.axis_size("col")
    scale = lax.rsqrt(degrees.astype(jnp.float32))
    scaled = (grad_out.astype(jnp.float32) * scale[:, None]).astype(jnp.bfloat16)
    owner = tile_owner[:, 0]
    weight_mine = weight_rows(weight)
    blocked = features.reshape(blocks, size, width)
    wide_scale = jnp.broadcast_to(scale.reshape(blocks, size, 1), (blocks, size, width))

    starts = [sum(SPLIT[:k]) for k in range(len(SPLIT))]
    gathered = lax.all_gather(features, "col", axis=0).reshape(cols, blocks, size, width)
    outgoing = [
        products(tile_row_block, owner, tile_local, live, tiles, scaled, peers, first, rows, k == 0)
        for k, (first, rows) in enumerate(zip(starts, SPLIT))
    ]
    outgoing[1], weight_mine, gathered = lax.optimization_barrier(
        (outgoing[1], weight_mine, gathered)
    )
    incoming = [exchange(each) for each in outgoing]

    tags = incoming[0][:, PLACES * SPLIT[0], :PLACES].astype(jnp.int32).reshape(-1)
    tags = jnp.where(tags < 0, blocks, tags)
    scales = [wide_scale[:, first : first + rows] for first, rows in zip(starts, SPLIT)]
    grad_pre = None
    terms = jnp.zeros((cols, width, width), jnp.float32)
    for k, (first, rows) in enumerate(zip(starts, SPLIT)):
        if k > 0:
            incoming[k], grad_pre, terms, scales[k] = lax.optimization_barrier(
                (incoming[k], grad_pre, terms, scales[k])
            )
        low, high = sums(tags, incoming[k], scales[k], rows)
        low, high = col_gather(low, high)
        propagated = jnp.concatenate([low[0], high[0]], axis=0)
        terms = terms + lax.dot_general(
            gathered[:, :, first : first + rows],
            propagated,
            (((1, 2), (0, 1)), ((), ())),
            preferred_element_type=jnp.float32,
        )
        grad_pre = back(low, high, weight_mine, blocked, grad_pre, first, rows)

    norm_factor = 1.0 / math.sqrt(node_rows * peers)
    share = cols * width // peers
    total = jnp.sum(exchange(terms.reshape(peers, share, width)), axis=0) * norm_factor
    total = jnp.broadcast_to(total.astype(jnp.bfloat16)[None], (peers, share, width))
    grad_weight = exchange(total).astype(jnp.float32)
    return (grad_pre.reshape(node_rows, width), grad_weight.reshape(cols * width, width))


def solution(mesh):
    return jax.shard_map(
        per_device,
        mesh=mesh,
        in_specs=(
            P("row", "col"),
            P("row", "col"),
            P(None, "col"),
            P("row", None, None),
            P("row"),
            P("row", None),
            P("row"),
            P("row"),
            P("row"),
        ),
        out_specs=(P("row", "col"), P(None, "col")),
        check_vma=False,
    )
```

```python
import functools
import math

import jax
import jax.numpy as jnp
from jax import lax
from jax.experimental import pallas as pl
from jax.experimental.pallas import tpu as pltpu
from jax.sharding import PartitionSpec as P

PLACES = 4
LABEL_ROWS = 8
SPLIT = (80, 48)
VMEM_PRODUCTS = 54 * 1024 * 1024
VMEM_SUMS = 48 * 1024 * 1024
VMEM_BACK = 16 * 1024 * 1024


def product_kernel(
    row_block, owner, local, live, tiles, scaled, out, held, count, labels, arrived, *, first, rows, label
):
    groups, group, size, _ = held.shape

    def fetch(step):
        part = tiles.at[pl.ds(step * group, group)]
        return pltpu.make_async_copy(part, held.at[step], arrived.at[step])

    for step in range(groups):
        fetch(step).start()

    def clear(i, carry):
        count[i] = 0
        return carry

    lax.fori_loop(0, out.shape[0], clear, 0)
    if label:
        labels[...] = jnp.full(labels.shape, -1.0, labels.dtype)
    lane = lax.broadcasted_iota(jnp.int32, (LABEL_ROWS, size), 1)

    def multiply(step, carry):
        fetch(step).wait()
        for i in range(group):
            tile = step * group + i
            peer = owner[tile]
            place = count[peer]
            count[peer] = place + 1
            source = scaled[pl.ds(pl.multiple_of(row_block[tile] * size, size), size), :]
            product = lax.dot_general(
                held[step, i, :, first : first + rows],
                source,
                (((0,), (0,)), ((), ())),
                preferred_element_type=jnp.float32,
            )
            spot = pl.ds(pl.multiple_of(place * rows, rows), rows)
            out[peer, spot, :] = product.astype(out.dtype)
            if label:
                value = jnp.where(tile < live[0], local[tile], -1).astype(jnp.float32)
                old = labels[peer].astype(jnp.float32)
                labels[peer] = jnp.where(lane == place, value, old).astype(labels.dtype)
        return carry

    lax.fori_loop(0, groups, multiply, 0)
    if label:
        out[:, PLACES * rows :, :] = labels[...]


def products(row_block, owner, local, live, tiles, scaled, peers, first, rows, label):
    tile_count, size, _ = tiles.shape
    width = scaled.shape[1]
    group = 16
    groups = tile_count // group
    extra = LABEL_ROWS if label else 0
    scalars = [pl.BlockSpec(memory_space=pltpu.SMEM)] * 4
    return pl.pallas_call(
        functools.partial(product_kernel, first=first, rows=rows, label=label),
        in_specs=scalars
        + [pl.BlockSpec(memory_space=pltpu.HBM), pl.BlockSpec(memory_space=pltpu.VMEM)],
        out_specs=pl.BlockSpec(memory_space=pltpu.VMEM),
        scratch_shapes=[
            pltpu.VMEM((groups, group, size, size), jnp.bfloat16),
            pltpu.SMEM((peers,), jnp.int32),
            pltpu.VMEM((peers, LABEL_ROWS, width), jnp.bfloat16),
            pltpu.SemaphoreType.DMA((groups,)),
        ],
        out_shape=jax.ShapeDtypeStruct((peers, PLACES * rows + extra, width), jnp.bfloat16),
        compiler_params=pltpu.CompilerParams(vmem_limit_bytes=VMEM_PRODUCTS),
        cost_estimate=pl.CostEstimate(
            flops=2 * tile_count * size * rows * width,
            bytes_accessed=2 * tiles.size + 2 * scaled.size + 2 * peers * PLACES * rows * width,
            transcendentals=0,
        ),
        name="products",
    )(row_block, owner, local, live, tiles, scaled)


def sum_kernel(labels, incoming, scale, low, high, total, held, arrived, *, rows):
    half = low.shape[0]
    groups, group = held.shape[:2]

    def fetch(step):
        part = incoming.at[pl.ds(step * group, group)]
        return pltpu.make_async_copy(part, held.at[step], arrived.at[step])

    for step in range(groups):
        fetch(step).start()
    total[...] = jnp.zeros_like(total)

    def add(step, carry):
        fetch(step).wait()
        for i in range(group):
            for place in range(PLACES):
                block = labels[(step * group + i) * PLACES + place]
                slot = held[step, i, place * rows : (place + 1) * rows, :]
                total[block] += slot.astype(jnp.float32)
        return carry

    lax.fori_loop(0, groups, add, 0)
    low[...] = (total[:half] * scale[:half]).astype(low.dtype)
    high[...] = (total[half : 2 * half] * scale[half:]).astype(high.dtype)


def sums(labels, incoming, scale, rows):
    peers, depth, width = incoming.shape
    blocks = scale.shape[0]
    group = 8
    vmem = pl.BlockSpec(memory_space=pltpu.VMEM)
    return pl.pallas_call(
        functools.partial(sum_kernel, rows=rows),
        in_specs=[
            pl.BlockSpec(memory_space=pltpu.SMEM),
            pl.BlockSpec(memory_space=pltpu.HBM),
            vmem,
        ],
        out_specs=[vmem] * 2,
        scratch_shapes=[
            pltpu.VMEM((blocks + 1, rows, width), jnp.float32),
            pltpu.VMEM((peers // group, group, depth, width), jnp.bfloat16),
            pltpu.SemaphoreType.DMA((peers // group,)),
        ],
        out_shape=[jax.ShapeDtypeStruct((blocks // 2, rows, width), jnp.bfloat16)] * 2,
        compiler_params=pltpu.CompilerParams(vmem_limit_bytes=VMEM_SUMS),
        cost_estimate=pl.CostEstimate(
            flops=incoming.size,
            bytes_accessed=2 * incoming.size + 4 * scale.size + 2 * scale.size,
            transcendentals=0,
        ),
        name="sums",
    )(labels, incoming, scale)


def back_kernel(*refs, half, first, rows):
    low, high, (weight, features), out = refs[:4], refs[4:8], refs[8:10], refs[-1]
    group, width = features.shape[0], features.shape[2]

    def run(parts):
        whole = jnp.concatenate([part[...].reshape(group * rows, width) for part in parts], axis=1)
        back = lax.dot_general(
            whole, weight[...], (((1,), (0,)), ((), ())), preferred_element_type=jnp.float32
        ).reshape(group, rows, width)
        mask = features[:, first : first + rows, :].astype(jnp.float32) > 0
        out[:, first : first + rows, :] = jnp.where(mask, back, 0.0).astype(out.dtype)

    if first:
        out[:, :first, :] = refs[10][...]

    @pl.when(pl.program_id(0) < half)
    def _():
        run(low)

    @pl.when(pl.program_id(0) >= half)
    def _():
        run(high)


def back(low, high, weight, features, before, first, rows):
    blocks, size, width = features.shape
    steps = 4
    group = blocks // steps
    half = steps // 2
    specs = [pl.BlockSpec((group, rows, width), lambda i: (jnp.minimum(i, half - 1), 0, 0))] * 4
    specs += [pl.BlockSpec((group, rows, width), lambda i: (jnp.maximum(i - half, 0), 0, 0))] * 4
    specs += [
        pl.BlockSpec(weight.shape, lambda i: (0, 0)),
        pl.BlockSpec((group, size, width), lambda i: (i, 0, 0)),
    ]
    args = [*low, *high, weight, features]
    if first:
        specs.append(pl.BlockSpec((group, first, width), lambda i: (i, 0, 0)))
        args.append(before)
    return pl.pallas_call(
        functools.partial(back_kernel, half=half, first=first, rows=rows),
        grid=(steps,),
        in_specs=specs,
        out_specs=pl.BlockSpec((group, first + rows, width), lambda i: (i, 0, 0)),
        out_shape=jax.ShapeDtypeStruct((blocks, first + rows, width), jnp.bfloat16),
        compiler_params=pltpu.CompilerParams(vmem_limit_bytes=VMEM_BACK),
        cost_estimate=pl.CostEstimate(
            flops=2 * blocks * rows * width * weight.shape[0],
            bytes_accessed=2 * blocks * rows * (weight.shape[0] + 2 * width),
            transcendentals=0,
        ),
        name="back",
    )(*args)


def ring(shift, size):
    return [(i, (i + shift) % size) for i in range(size)]


def exchange(block):
    return lax.all_to_all(block, "row", split_axis=0, concat_axis=0, tiled=True)


def col_near(low, high):
    ahead, behind = ring(1, lax.axis_size("col")), ring(-1, lax.axis_size("col"))
    low_left = lax.ppermute(low, "col", ahead)
    high_right = lax.ppermute(high, "col", behind)
    high_left = lax.ppermute(high, "col", ahead)
    low_right = lax.ppermute(low, "col", behind)
    return low_left, high_left, low_right, high_right


def col_far(low_left, high_right):
    size = lax.axis_size("col")
    return (
        lax.ppermute(low_left, "col", ring(1, size)),
        lax.ppermute(high_right, "col", ring(-1, size)),
    )


def pair_up(own, near, far):
    low = (own[0], near[0], far[0], near[2])
    high = (own[1], near[1], far[1], near[3])
    return low, high


def weight_rows(weight):
    size = lax.axis_size("col")
    width = weight.shape[1]
    me = lax.axis_index("col")
    parts = []
    for shift in range(size):
        start = lax.rem(me + shift, size) * width
        slab = lax.dynamic_slice_in_dim(weight, start, width, 0)
        parts.append(slab if shift == 0 else lax.ppermute(slab, "col", ring(shift, size)))
    return jnp.concatenate(parts, axis=1).T


def per_device(
    grad_out, features, weight, tiles, tile_row_block, tile_owner, tile_local, degrees, live
):
    node_rows, width = grad_out.shape
    size = tiles.shape[1]
    blocks = node_rows // size
    peers = lax.axis_size("row")
    cols = lax.axis_size("col")
    scale = lax.rsqrt(degrees.astype(jnp.float32))
    scaled = (grad_out.astype(jnp.float32) * scale[:, None]).astype(jnp.bfloat16)
    owner = tile_owner[:, 0]
    weight_mine = weight_rows(weight)
    blocked = features.reshape(blocks, size, width)
    wide_scale = jnp.broadcast_to(scale.reshape(blocks, size, 1), (blocks, size, width))

    starts = [sum(SPLIT[:k]) for k in range(len(SPLIT))]
    gathered = lax.all_gather(features, "col", axis=0).reshape(cols, blocks, size, width)
    outgoing = [
        products(tile_row_block, owner, tile_local, live, tiles, scaled, peers, first, rows, k == 0)
        for k, (first, rows) in enumerate(zip(starts, SPLIT))
    ]
    outgoing[1], weight_mine, gathered = lax.optimization_barrier(
        (outgoing[1], weight_mine, gathered)
    )
    incoming = [exchange(each) for each in outgoing]

    tags = incoming[0][:, PLACES * SPLIT[0], :PLACES].astype(jnp.int32).reshape(-1)
    tags = jnp.where(tags < 0, blocks, tags)
    scales = [wide_scale[:, first : first + rows] for first, rows in zip(starts, SPLIT)]

    def local_terms(own, first, rows):
        return lax.dot_general(
            gathered[:, :, first : first + rows],
            jnp.concatenate(own, axis=0),
            (((1, 2), (0, 1)), ((), ())),
            preferred_element_type=jnp.float32,
        )

    own = sums(tags, incoming[0], scales[0], SPLIT[0])
    near = col_near(*own)
    far = col_far(near[0], near[3])
    terms = local_terms(own, 0, SPLIT[0])
    before = back(*pair_up(own, near, far), weight_mine, blocked, None, 0, SPLIT[0])
    incoming[1], scales[1], terms, before = lax.optimization_barrier(
        (incoming[1], scales[1], terms, before)
    )

    own = sums(tags, incoming[1], scales[1], SPLIT[1])
    near = col_near(*own)
    terms = terms + local_terms(own, *SPLIT)
    norm_factor = 1.0 / math.sqrt(node_rows * peers)
    share = cols * width // peers
    total = jnp.sum(exchange(terms.reshape(peers, share, width)), axis=0) * norm_factor
    total = jnp.broadcast_to(total.astype(jnp.bfloat16)[None], (peers, share, width))
    near, _ = lax.optimization_barrier((near, total))
    far = col_far(near[0], near[3])
    grad_pre = back(*pair_up(own, near, far), weight_mine, blocked, before, *SPLIT)
    grad_weight = exchange(total).astype(jnp.float32)
    return (grad_pre.reshape(node_rows, width), grad_weight.reshape(cols * width, width))


def solution(mesh):
    return jax.shard_map(
        per_device,
        mesh=mesh,
        in_specs=(
            P("row", "col"),
            P("row", "col"),
            P(None, "col"),
            P("row", None, None),
            P("row"),
            P("row", None),
            P("row"),
            P("row"),
            P("row"),
        ),
        out_specs=(P("row", "col"), P(None, "col")),
        check_vma=False,
    )
```

```python
import functools
import math

import jax
import jax.numpy as jnp
from jax import lax
from jax.experimental import pallas as pl
from jax.experimental.pallas import tpu as pltpu
from jax.sharding import PartitionSpec as P

PLACES = 4
LABEL_ROWS = 8
STRIP = 16
SPLIT = (80, 48)
VMEM_PRODUCTS = 54 * 1024 * 1024
VMEM_SUMS = 48 * 1024 * 1024
VMEM_BACK = 16 * 1024 * 1024


def product_kernel(
    row_block, owner, local, live, tiles, scaled, out, held, count, labels, arrived, *, first, rows, label
):
    groups, group, size, _ = held.shape

    def fetch(step):
        part = tiles.at[pl.ds(step * group, group)]
        return pltpu.make_async_copy(part, held.at[step], arrived.at[step])

    for step in range(groups):
        fetch(step).start()

    def clear(i, carry):
        count[i] = 0
        return carry

    lax.fori_loop(0, out.shape[0], clear, 0)
    if label:
        labels[...] = jnp.full(labels.shape, -1.0, labels.dtype)
    lane = lax.broadcasted_iota(jnp.int32, (LABEL_ROWS, size), 1)

    def multiply(step, carry):
        fetch(step).wait()
        for i in range(group):
            tile = step * group + i
            peer = owner[tile]
            place = count[peer]
            count[peer] = place + 1
            source = scaled[pl.ds(pl.multiple_of(row_block[tile] * size, size), size), :]
            product = lax.dot_general(
                held[step, i, :, first : first + rows],
                source,
                (((0,), (0,)), ((), ())),
                preferred_element_type=jnp.float32,
            )
            spot = pl.ds(pl.multiple_of(place * rows, rows), rows)
            out[peer, spot, :] = product.astype(out.dtype)
            if label:
                value = jnp.where(tile < live[0], local[tile], -1).astype(jnp.float32)
                old = labels[peer].astype(jnp.float32)
                labels[peer] = jnp.where(lane == place, value, old).astype(labels.dtype)
        return carry

    lax.fori_loop(0, groups, multiply, 0)
    if label:
        out[:, PLACES * rows :, :] = labels[...]


def products(row_block, owner, local, live, tiles, scaled, peers, first, rows, label):
    tile_count, size, _ = tiles.shape
    width = scaled.shape[1]
    group = 16
    groups = tile_count // group
    extra = LABEL_ROWS if label else 0
    scalars = [pl.BlockSpec(memory_space=pltpu.SMEM)] * 4
    return pl.pallas_call(
        functools.partial(product_kernel, first=first, rows=rows, label=label),
        in_specs=scalars
        + [pl.BlockSpec(memory_space=pltpu.HBM), pl.BlockSpec(memory_space=pltpu.VMEM)],
        out_specs=pl.BlockSpec(memory_space=pltpu.VMEM),
        scratch_shapes=[
            pltpu.VMEM((groups, group, size, size), jnp.bfloat16),
            pltpu.SMEM((peers,), jnp.int32),
            pltpu.VMEM((peers, LABEL_ROWS, width), jnp.bfloat16),
            pltpu.SemaphoreType.DMA((groups,)),
        ],
        out_shape=jax.ShapeDtypeStruct((peers, PLACES * rows + extra, width), jnp.bfloat16),
        compiler_params=pltpu.CompilerParams(vmem_limit_bytes=VMEM_PRODUCTS),
        cost_estimate=pl.CostEstimate(
            flops=2 * tile_count * size * rows * width,
            bytes_accessed=2 * tiles.size + 2 * scaled.size + 2 * peers * PLACES * rows * width,
            transcendentals=0,
        ),
        name="products",
    )(row_block, owner, local, live, tiles, scaled)


def sum_kernel(labels, incoming, scale, low, high, total, held, wide, arrived, *, rows):
    half = low.shape[0]
    groups, group = held.shape[:2]

    def fetch(step):
        part = incoming.at[pl.ds(step * group, group)]
        return pltpu.make_async_copy(part, held.at[step], arrived.at[step])

    for step in range(groups):
        fetch(step).start()
    total[...] = jnp.zeros_like(total)
    own_lane = lax.broadcasted_iota(jnp.int32, (rows, rows), 0) == lax.broadcasted_iota(
        jnp.int32, (rows, rows), 1
    )

    def widen(i, carry):
        for j in range(4):
            block = i * 4 + j
            row = scale[pl.ds(block, 1), :]
            column = jnp.sum(jnp.where(own_lane, row, 0.0), axis=1, keepdims=True)
            wide[block] = jnp.broadcast_to(column, wide.shape[1:])
        return carry

    lax.fori_loop(0, wide.shape[0] // 4, widen, 0)

    def add(step, carry):
        fetch(step).wait()
        for i in range(group):
            for place in range(PLACES):
                block = labels[(step * group + i) * PLACES + place]
                slot = held[step, i, place * rows : (place + 1) * rows, :]
                total[block] += slot.astype(jnp.float32)
        return carry

    lax.fori_loop(0, groups, add, 0)
    low[...] = (total[:half] * wide[:half]).astype(low.dtype)
    high[...] = (total[half : 2 * half] * wide[half:]).astype(high.dtype)


def sums(labels, incoming, scale, rows):
    peers, depth, width = incoming.shape
    blocks = scale.shape[0]
    group = 8
    vmem = pl.BlockSpec(memory_space=pltpu.VMEM)
    return pl.pallas_call(
        functools.partial(sum_kernel, rows=rows),
        in_specs=[
            pl.BlockSpec(memory_space=pltpu.SMEM),
            pl.BlockSpec(memory_space=pltpu.HBM),
            vmem,
        ],
        out_specs=[vmem] * 2,
        scratch_shapes=[
            pltpu.VMEM((blocks + 1, rows, width), jnp.float32),
            pltpu.VMEM((peers // group, group, depth, width), jnp.bfloat16),
            pltpu.VMEM((blocks, rows, width), jnp.float32),
            pltpu.SemaphoreType.DMA((peers // group,)),
        ],
        out_shape=[jax.ShapeDtypeStruct((blocks // 2, rows, width), jnp.bfloat16)] * 2,
        compiler_params=pltpu.CompilerParams(vmem_limit_bytes=VMEM_SUMS),
        cost_estimate=pl.CostEstimate(
            flops=incoming.size,
            bytes_accessed=2 * incoming.size + 2 * scale.size * width,
            transcendentals=0,
        ),
        name="sums",
    )(labels, incoming, scale)


def back_kernel(*refs):
    low, high, (weight, features), out = refs[:4], refs[4:8], refs[8:10], refs[-1]
    half, _, strip, width = features.shape

    def run(parts):
        whole = jnp.concatenate([part[...].reshape(half * strip, width) for part in parts], axis=1)
        back = lax.dot_general(
            whole, weight[...], (((1,), (0,)), ((), ())), preferred_element_type=jnp.float32
        ).reshape(features.shape)
        mask = features[...].astype(jnp.float32) > 0
        out[...] = jnp.where(mask, back, 0.0).astype(out.dtype)

    @pl.when(pl.program_id(0) == 0)
    def _():
        run(low)

    @pl.when(pl.program_id(0) == 1)
    def _():
        run(high)


def back(low, high, weight, features, before, first, rows):
    blocks, strips, strip, width = features.shape
    half, steps, skip = blocks // 2, rows // strip, first // strip
    piece = pl.BlockSpec((half, 1, strip, width), lambda i, j: (i, skip + j, 0, 0))
    specs = [
        pl.BlockSpec((half, strip, width), lambda i, j: (0, jnp.where(i == 0, j, steps - 1), 0))
    ] * 4
    specs += [pl.BlockSpec((half, strip, width), lambda i, j: (0, jnp.where(i == 0, 0, j), 0))] * 4
    specs += [pl.BlockSpec(weight.shape, lambda i, j: (0, 0)), piece]
    args = [*low, *high, weight, features]
    aliases = {}
    if before is not None:
        specs.append(pl.BlockSpec(memory_space=pl.ANY))
        args.append(before)
        aliases = {len(args) - 1: 0}
    return pl.pallas_call(
        back_kernel,
        grid=(2, steps),
        in_specs=specs,
        out_specs=piece,
        out_shape=jax.ShapeDtypeStruct(features.shape, jnp.bfloat16),
        input_output_aliases=aliases,
        compiler_params=pltpu.CompilerParams(vmem_limit_bytes=VMEM_BACK),
        cost_estimate=pl.CostEstimate(
            flops=2 * blocks * rows * width * weight.shape[0],
            bytes_accessed=2 * blocks * rows * (weight.shape[0] + 2 * width),
            transcendentals=0,
        ),
        name="back",
    )(*args)


def ring(shift, size):
    return [(i, (i + shift) % size) for i in range(size)]


def exchange(block):
    return lax.all_to_all(block, "row", split_axis=0, concat_axis=0, tiled=True)


def col_near(low, high):
    ahead, behind = ring(1, lax.axis_size("col")), ring(-1, lax.axis_size("col"))
    low_left = lax.ppermute(low, "col", ahead)
    high_right = lax.ppermute(high, "col", behind)
    high_left = lax.ppermute(high, "col", ahead)
    low_right = lax.ppermute(low, "col", behind)
    return low_left, high_left, low_right, high_right


def col_far(low_left, high_right):
    size = lax.axis_size("col")
    return (
        lax.ppermute(low_left, "col", ring(1, size)),
        lax.ppermute(high_right, "col", ring(-1, size)),
    )


def pair_up(own, near, far):
    low = (own[0], near[0], far[0], near[2])
    high = (own[1], near[1], far[1], near[3])
    return low, high


def weight_rows(weight):
    size = lax.axis_size("col")
    width = weight.shape[1]
    me = lax.axis_index("col")
    parts = []
    for shift in range(size):
        start = lax.rem(me + shift, size) * width
        slab = lax.dynamic_slice_in_dim(weight, start, width, 0)
        parts.append(slab if shift == 0 else lax.ppermute(slab, "col", ring(shift, size)))
    return jnp.concatenate(parts, axis=1).T


def per_device(
    grad_out, features, weight, tiles, tile_row_block, tile_owner, tile_local, degrees, live
):
    node_rows, width = grad_out.shape
    size = tiles.shape[1]
    blocks = node_rows // size
    peers = lax.axis_size("row")
    cols = lax.axis_size("col")
    scale = lax.rsqrt(degrees.astype(jnp.float32))
    scaled = (grad_out.astype(jnp.float32) * scale[:, None]).astype(jnp.bfloat16)
    owner = tile_owner[:, 0]
    weight_mine = weight_rows(weight)
    blocked = features.reshape(blocks, size // STRIP, STRIP, width)
    block_scale = scale.reshape(blocks, size)

    starts = [sum(SPLIT[:k]) for k in range(len(SPLIT))]
    gathered = lax.all_gather(features, "col", axis=0).reshape(cols, blocks, size, width)
    outgoing = [
        products(tile_row_block, owner, tile_local, live, tiles, scaled, peers, first, rows, k == 0)
        for k, (first, rows) in enumerate(zip(starts, SPLIT))
    ]
    outgoing[1], weight_mine, gathered = lax.optimization_barrier(
        (outgoing[1], weight_mine, gathered)
    )
    incoming = [exchange(each) for each in outgoing]

    tags = incoming[0][:, PLACES * SPLIT[0], :PLACES].astype(jnp.int32).reshape(-1)
    tags = jnp.where(tags < 0, blocks, tags)
    scales = [block_scale[:, first : first + rows] for first, rows in zip(starts, SPLIT)]

    def local_terms(own, first, rows):
        return lax.dot_general(
            gathered[:, :, first : first + rows],
            jnp.concatenate(own, axis=0),
            (((1, 2), (0, 1)), ((), ())),
            preferred_element_type=jnp.float32,
        )

    own = sums(tags, incoming[0], scales[0], SPLIT[0])
    near = col_near(*own)
    far = col_far(near[0], near[3])
    terms = local_terms(own, 0, SPLIT[0])
    before = back(*pair_up(own, near, far), weight_mine, blocked, None, 0, SPLIT[0])
    incoming[1], scales[1], terms, before = lax.optimization_barrier(
        (incoming[1], scales[1], terms, before)
    )

    own = sums(tags, incoming[1], scales[1], SPLIT[1])
    near = col_near(*own)
    terms = terms + local_terms(own, *SPLIT)
    norm_factor = 1.0 / math.sqrt(node_rows * peers)
    share = cols * width // peers
    pieces = exchange(terms.reshape(peers, share, width).astype(jnp.bfloat16))
    total = jnp.sum(pieces.astype(jnp.float32), axis=0) * norm_factor
    total = jnp.broadcast_to(total.astype(jnp.bfloat16)[None], (peers, share, width))
    near, _ = lax.optimization_barrier((near, total))
    far = col_far(near[0], near[3])
    grad_pre = back(*pair_up(own, near, far), weight_mine, blocked, before, *SPLIT)
    grad_weight = exchange(total).astype(jnp.float32)
    return (grad_pre.reshape(node_rows, width), grad_weight.reshape(cols * width, width))


def solution(mesh):
    return jax.shard_map(
        per_device,
        mesh=mesh,
        in_specs=(
            P("row", "col"),
            P("row", "col"),
            P(None, "col"),
            P("row", None, None),
            P("row"),
            P("row", None),
            P("row"),
            P("row"),
            P("row"),
        ),
        out_specs=(P("row", "col"), P(None, "col")),
        check_vma=False,
    )
```

```python
import functools
import math

import jax
import jax.numpy as jnp
from jax import lax
from jax.experimental import pallas as pl
from jax.experimental.pallas import tpu as pltpu
from jax.sharding import PartitionSpec as P

PLACES = 4
LABEL_ROWS = 8
STRIP = 16
BACK_STEPS = 4
SPLIT = (80, 48)
VMEM_PRODUCTS = 54 * 1024 * 1024
VMEM_SUMS = 48 * 1024 * 1024
VMEM_BACK = 16 * 1024 * 1024


def product_kernel(
    row_block, owner, local, live, tiles, scaled, out, held, count, labels, arrived, *, first, rows, label
):
    groups, group, size, _ = held.shape

    def fetch(step):
        part = tiles.at[pl.ds(step * group, group)]
        return pltpu.make_async_copy(part, held.at[step], arrived.at[step])

    for step in range(groups):
        fetch(step).start()

    def clear(i, carry):
        count[i] = 0
        return carry

    lax.fori_loop(0, out.shape[0], clear, 0)
    if label:
        labels[...] = jnp.full(labels.shape, -1.0, labels.dtype)
    lane = lax.broadcasted_iota(jnp.int32, (LABEL_ROWS, size), 1)

    def multiply(step, carry):
        fetch(step).wait()
        for i in range(group):
            tile = step * group + i
            peer = owner[tile]
            place = count[peer]
            count[peer] = place + 1
            source = scaled[pl.ds(pl.multiple_of(row_block[tile] * size, size), size), :]
            product = lax.dot_general(
                held[step, i, :, first : first + rows],
                source,
                (((0,), (0,)), ((), ())),
                preferred_element_type=jnp.float32,
            )
            spot = pl.ds(pl.multiple_of(place * rows, rows), rows)
            out[peer, spot, :] = product.astype(out.dtype)
            if label:
                value = jnp.where(tile < live[0], local[tile], -1).astype(jnp.float32)
                old = labels[peer].astype(jnp.float32)
                labels[peer] = jnp.where(lane == place, value, old).astype(labels.dtype)
        return carry

    lax.fori_loop(0, groups, multiply, 0)
    if label:
        out[:, PLACES * rows :, :] = labels[...]


def products(row_block, owner, local, live, tiles, scaled, peers, first, rows, label):
    tile_count, size, _ = tiles.shape
    width = scaled.shape[1]
    group = 16
    groups = tile_count // group
    extra = LABEL_ROWS if label else 0
    scalars = [pl.BlockSpec(memory_space=pltpu.SMEM)] * 4
    return pl.pallas_call(
        functools.partial(product_kernel, first=first, rows=rows, label=label),
        in_specs=scalars
        + [pl.BlockSpec(memory_space=pltpu.HBM), pl.BlockSpec(memory_space=pltpu.VMEM)],
        out_specs=pl.BlockSpec(memory_space=pltpu.VMEM),
        scratch_shapes=[
            pltpu.VMEM((groups, group, size, size), jnp.bfloat16),
            pltpu.SMEM((peers,), jnp.int32),
            pltpu.VMEM((peers, LABEL_ROWS, width), jnp.bfloat16),
            pltpu.SemaphoreType.DMA((groups,)),
        ],
        out_shape=jax.ShapeDtypeStruct((peers, PLACES * rows + extra, width), jnp.bfloat16),
        compiler_params=pltpu.CompilerParams(vmem_limit_bytes=VMEM_PRODUCTS),
        cost_estimate=pl.CostEstimate(
            flops=2 * tile_count * size * rows * width,
            bytes_accessed=2 * tiles.size + 2 * scaled.size + 2 * peers * PLACES * rows * width,
            transcendentals=0,
        ),
        name="products",
    )(row_block, owner, local, live, tiles, scaled)


def sum_kernel(labels, incoming, scale, low, high, total, held, wide, arrived, *, rows):
    half = low.shape[0]
    groups, group = held.shape[:2]

    def fetch(step):
        part = incoming.at[pl.ds(step * group, group)]
        return pltpu.make_async_copy(part, held.at[step], arrived.at[step])

    for step in range(groups):
        fetch(step).start()
    total[...] = jnp.zeros_like(total)
    own_lane = lax.broadcasted_iota(jnp.int32, (rows, rows), 0) == lax.broadcasted_iota(
        jnp.int32, (rows, rows), 1
    )

    def widen(i, carry):
        for j in range(4):
            block = i * 4 + j
            row = scale[pl.ds(block, 1), :]
            column = jnp.sum(jnp.where(own_lane, row, 0.0), axis=1, keepdims=True)
            wide[block] = jnp.broadcast_to(column, wide.shape[1:])
        return carry

    lax.fori_loop(0, wide.shape[0] // 4, widen, 0)

    def add(step, carry):
        fetch(step).wait()
        for i in range(group):
            for place in range(PLACES):
                block = labels[(step * group + i) * PLACES + place]
                slot = held[step, i, place * rows : (place + 1) * rows, :]
                total[block] += slot.astype(jnp.float32)
        return carry

    lax.fori_loop(0, groups, add, 0)
    low[...] = (total[:half] * wide[:half]).astype(low.dtype)
    high[...] = (total[half : 2 * half] * wide[half:]).astype(high.dtype)


def sums(labels, incoming, scale, rows):
    peers, depth, width = incoming.shape
    blocks = scale.shape[0]
    group = 8
    vmem = pl.BlockSpec(memory_space=pltpu.VMEM)
    return pl.pallas_call(
        functools.partial(sum_kernel, rows=rows),
        in_specs=[
            pl.BlockSpec(memory_space=pltpu.SMEM),
            pl.BlockSpec(memory_space=pltpu.HBM),
            vmem,
        ],
        out_specs=[vmem] * 2,
        scratch_shapes=[
            pltpu.VMEM((blocks + 1, rows, width), jnp.float32),
            pltpu.VMEM((peers // group, group, depth, width), jnp.bfloat16),
            pltpu.VMEM((blocks, rows, width), jnp.float32),
            pltpu.SemaphoreType.DMA((peers // group,)),
        ],
        out_shape=[jax.ShapeDtypeStruct((blocks // 2, rows, width), jnp.bfloat16)] * 2,
        compiler_params=pltpu.CompilerParams(vmem_limit_bytes=VMEM_SUMS),
        cost_estimate=pl.CostEstimate(
            flops=incoming.size,
            bytes_accessed=2 * incoming.size + 2 * scale.size * width,
            transcendentals=0,
        ),
        name="sums",
    )(labels, incoming, scale)


def back_kernel(*refs, half):
    low, high, (weight, features), out = refs[:4], refs[4:8], refs[8:10], refs[-1]
    group, strips, strip, width = features.shape
    nodes = group * strips * strip

    def run(parts):
        whole = jnp.concatenate([part[...].reshape(nodes, width) for part in parts], axis=1)
        back = lax.dot_general(
            whole, weight[...], (((1,), (0,)), ((), ())), preferred_element_type=jnp.float32
        ).reshape(features.shape)
        mask = features[...].astype(jnp.float32) > 0
        out[...] = jnp.where(mask, back, 0.0).astype(out.dtype)

    @pl.when(pl.program_id(0) < half)
    def _():
        run(low)

    @pl.when(pl.program_id(0) >= half)
    def _():
        run(high)


def back(low, high, weight, features, before, first, rows):
    blocks, strips, strip, width = features.shape
    steps = BACK_STEPS
    group, half, skip = blocks // steps, steps // 2, first // strip
    piece = pl.BlockSpec(
        (pl.Element(group), pl.Element(rows // strip), pl.Element(strip), pl.Element(width)),
        lambda i: (i * group, skip, 0, 0),
    )
    specs = [pl.BlockSpec((group, rows, width), lambda i: (jnp.minimum(i, half - 1), 0, 0))] * 4
    specs += [pl.BlockSpec((group, rows, width), lambda i: (jnp.maximum(i - half, 0), 0, 0))] * 4
    specs += [pl.BlockSpec(weight.shape, lambda i: (0, 0)), piece]
    args = [*low, *high, weight, features]
    aliases = {}
    if before is not None:
        specs.append(pl.BlockSpec(memory_space=pl.ANY))
        args.append(before)
        aliases = {len(args) - 1: 0}
    return pl.pallas_call(
        functools.partial(back_kernel, half=half),
        grid=(steps,),
        in_specs=specs,
        out_specs=piece,
        out_shape=jax.ShapeDtypeStruct(features.shape, jnp.bfloat16),
        input_output_aliases=aliases,
        compiler_params=pltpu.CompilerParams(vmem_limit_bytes=VMEM_BACK),
        cost_estimate=pl.CostEstimate(
            flops=2 * blocks * rows * width * weight.shape[0],
            bytes_accessed=2 * blocks * rows * (weight.shape[0] + 2 * width),
            transcendentals=0,
        ),
        name="back",
    )(*args)


def ring(shift, size):
    return [(i, (i + shift) % size) for i in range(size)]


def exchange(block):
    return lax.all_to_all(block, "row", split_axis=0, concat_axis=0, tiled=True)


def col_near(low, high):
    ahead, behind = ring(1, lax.axis_size("col")), ring(-1, lax.axis_size("col"))
    low_left = lax.ppermute(low, "col", ahead)
    high_right = lax.ppermute(high, "col", behind)
    high_left = lax.ppermute(high, "col", ahead)
    low_right = lax.ppermute(low, "col", behind)
    return low_left, high_left, low_right, high_right


def col_far(low_left, high_right):
    size = lax.axis_size("col")
    return (
        lax.ppermute(low_left, "col", ring(1, size)),
        lax.ppermute(high_right, "col", ring(-1, size)),
    )


def pair_up(own, near, far):
    low = (own[0], near[0], far[0], near[2])
    high = (own[1], near[1], far[1], near[3])
    return low, high


def weight_rows(weight):
    size = lax.axis_size("col")
    width = weight.shape[1]
    me = lax.axis_index("col")
    parts = []
    for shift in range(size):
        start = lax.rem(me + shift, size) * width
        slab = lax.dynamic_slice_in_dim(weight, start, width, 0)
        parts.append(slab if shift == 0 else lax.ppermute(slab, "col", ring(shift, size)))
    return jnp.concatenate(parts, axis=1).T


def per_device(
    grad_out, features, weight, tiles, tile_row_block, tile_owner, tile_local, degrees, live
):
    node_rows, width = grad_out.shape
    size = tiles.shape[1]
    blocks = node_rows // size
    peers = lax.axis_size("row")
    cols = lax.axis_size("col")
    scale = lax.rsqrt(degrees.astype(jnp.float32))
    scaled = (grad_out.astype(jnp.float32) * scale[:, None]).astype(jnp.bfloat16)
    owner = tile_owner[:, 0]
    weight_mine = weight_rows(weight)
    blocked = features.reshape(blocks, size // STRIP, STRIP, width)
    block_scale = scale.reshape(blocks, size)

    starts = [sum(SPLIT[:k]) for k in range(len(SPLIT))]
    gathered = lax.all_gather(features, "col", axis=0).reshape(cols, blocks, size, width)
    outgoing = [
        products(tile_row_block, owner, tile_local, live, tiles, scaled, peers, first, rows, k == 0)
        for k, (first, rows) in enumerate(zip(starts, SPLIT))
    ]
    outgoing[1], weight_mine, gathered = lax.optimization_barrier(
        (outgoing[1], weight_mine, gathered)
    )
    incoming = [exchange(each) for each in outgoing]

    tags = incoming[0][:, PLACES * SPLIT[0], :PLACES].astype(jnp.int32).reshape(-1)
    tags = jnp.where(tags < 0, blocks, tags)
    scales = [block_scale[:, first : first + rows] for first, rows in zip(starts, SPLIT)]

    def local_terms(own, first, rows):
        return lax.dot_general(
            gathered[:, :, first : first + rows],
            jnp.concatenate(own, axis=0),
            (((1, 2), (0, 1)), ((), ())),
            preferred_element_type=jnp.float32,
        )

    own = sums(tags, incoming[0], scales[0], SPLIT[0])
    near = col_near(*own)
    far = col_far(near[0], near[3])
    terms = local_terms(own, 0, SPLIT[0])
    before = back(*pair_up(own, near, far), weight_mine, blocked, None, 0, SPLIT[0])
    incoming[1], scales[1], terms, before = lax.optimization_barrier(
        (incoming[1], scales[1], terms, before)
    )

    own = sums(tags, incoming[1], scales[1], SPLIT[1])
    near = col_near(*own)
    terms = terms + local_terms(own, *SPLIT)
    norm_factor = 1.0 / math.sqrt(node_rows * peers)
    share = cols * width // peers
    pieces = exchange(terms.reshape(peers, share, width).astype(jnp.bfloat16))
    total = jnp.sum(pieces.astype(jnp.float32), axis=0) * norm_factor
    total = jnp.broadcast_to(total.astype(jnp.bfloat16)[None], (peers, share, width))
    near, _ = lax.optimization_barrier((near, total))
    far = col_far(near[0], near[3])
    grad_pre = back(*pair_up(own, near, far), weight_mine, blocked, before, *SPLIT)
    grad_weight = exchange(total).astype(jnp.float32)
    return (grad_pre.reshape(node_rows, width), grad_weight.reshape(cols * width, width))


def solution(mesh):
    return jax.shard_map(
        per_device,
        mesh=mesh,
        in_specs=(
            P("row", "col"),
            P("row", "col"),
            P(None, "col"),
            P("row", None, None),
            P("row"),
            P("row", None),
            P("row"),
            P("row"),
            P("row"),
        ),
        out_specs=(P("row", "col"), P(None, "col")),
        check_vma=False,
    )
```

```python
import functools
import math

import jax
import jax.numpy as jnp
from jax import lax
from jax.experimental import pallas as pl
from jax.experimental.pallas import tpu as pltpu
from jax.sharding import PartitionSpec as P

PLACES = 4
LABEL_ROWS = 8
STRIP = 16
BACK_STEPS = 4
SPLIT = (96, 32)
VMEM_PRODUCTS = 54 * 1024 * 1024
VMEM_SUMS = 48 * 1024 * 1024
VMEM_BACK = 16 * 1024 * 1024


def product_kernel(
    row_block, owner, local, live, tiles, scaled, out, held, count, labels, arrived, *, first, rows, label
):
    groups, group, size, _ = held.shape

    def fetch(step):
        part = tiles.at[pl.ds(step * group, group)]
        return pltpu.make_async_copy(part, held.at[step], arrived.at[step])

    for step in range(groups):
        fetch(step).start()

    def clear(i, carry):
        count[i] = 0
        return carry

    lax.fori_loop(0, out.shape[0], clear, 0)
    if label:
        labels[...] = jnp.full(labels.shape, -1.0, labels.dtype)
    lane = lax.broadcasted_iota(jnp.int32, (LABEL_ROWS, size), 1)

    def multiply(step, carry):
        fetch(step).wait()
        for i in range(group):
            tile = step * group + i
            peer = owner[tile]
            place = count[peer]
            count[peer] = place + 1
            source = scaled[pl.ds(pl.multiple_of(row_block[tile] * size, size), size), :]
            product = lax.dot_general(
                held[step, i, :, first : first + rows],
                source,
                (((0,), (0,)), ((), ())),
                preferred_element_type=jnp.float32,
            )
            spot = pl.ds(pl.multiple_of(place * rows, rows), rows)
            out[peer, spot, :] = product.astype(out.dtype)
            if label:
                value = jnp.where(tile < live[0], local[tile], -1).astype(jnp.float32)
                old = labels[peer].astype(jnp.float32)
                labels[peer] = jnp.where(lane == place, value, old).astype(labels.dtype)
        return carry

    lax.fori_loop(0, groups, multiply, 0)
    if label:
        out[:, PLACES * rows :, :] = labels[...]


def products(row_block, owner, local, live, tiles, scaled, peers, first, rows, label):
    tile_count, size, _ = tiles.shape
    width = scaled.shape[1]
    group = 16
    groups = tile_count // group
    extra = LABEL_ROWS if label else 0
    scalars = [pl.BlockSpec(memory_space=pltpu.SMEM)] * 4
    return pl.pallas_call(
        functools.partial(product_kernel, first=first, rows=rows, label=label),
        in_specs=scalars
        + [pl.BlockSpec(memory_space=pltpu.HBM), pl.BlockSpec(memory_space=pltpu.VMEM)],
        out_specs=pl.BlockSpec(memory_space=pltpu.VMEM),
        scratch_shapes=[
            pltpu.VMEM((groups, group, size, size), jnp.bfloat16),
            pltpu.SMEM((peers,), jnp.int32),
            pltpu.VMEM((peers, LABEL_ROWS, width), jnp.bfloat16),
            pltpu.SemaphoreType.DMA((groups,)),
        ],
        out_shape=jax.ShapeDtypeStruct((peers, PLACES * rows + extra, width), jnp.bfloat16),
        compiler_params=pltpu.CompilerParams(vmem_limit_bytes=VMEM_PRODUCTS),
        cost_estimate=pl.CostEstimate(
            flops=2 * tile_count * size * rows * width,
            bytes_accessed=2 * tiles.size + 2 * scaled.size + 2 * peers * PLACES * rows * width,
            transcendentals=0,
        ),
        name="products",
    )(row_block, owner, local, live, tiles, scaled)


def sum_kernel(labels, incoming, scale, low, high, total, held, wide, arrived, *, rows):
    half = low.shape[0]
    groups, group = held.shape[:2]

    def fetch(step):
        part = incoming.at[pl.ds(step * group, group)]
        return pltpu.make_async_copy(part, held.at[step], arrived.at[step])

    for step in range(groups):
        fetch(step).start()
    total[...] = jnp.zeros_like(total)
    own_lane = lax.broadcasted_iota(jnp.int32, (rows, rows), 0) == lax.broadcasted_iota(
        jnp.int32, (rows, rows), 1
    )

    def widen(i, carry):
        for j in range(4):
            block = i * 4 + j
            row = scale[pl.ds(block, 1), :]
            column = jnp.sum(jnp.where(own_lane, row, 0.0), axis=1, keepdims=True)
            wide[block] = jnp.broadcast_to(column, wide.shape[1:])
        return carry

    lax.fori_loop(0, wide.shape[0] // 4, widen, 0)

    def add(step, carry):
        fetch(step).wait()
        for i in range(group):
            for place in range(PLACES):
                block = labels[(step * group + i) * PLACES + place]
                slot = held[step, i, place * rows : (place + 1) * rows, :]
                total[block] += slot.astype(jnp.float32)
        return carry

    lax.fori_loop(0, groups, add, 0)
    low[...] = (total[:half] * wide[:half]).astype(low.dtype)
    high[...] = (total[half : 2 * half] * wide[half:]).astype(high.dtype)


def sums(labels, incoming, scale, rows):
    peers, depth, width = incoming.shape
    blocks = scale.shape[0]
    group = 8
    vmem = pl.BlockSpec(memory_space=pltpu.VMEM)
    return pl.pallas_call(
        functools.partial(sum_kernel, rows=rows),
        in_specs=[
            pl.BlockSpec(memory_space=pltpu.SMEM),
            pl.BlockSpec(memory_space=pltpu.HBM),
            vmem,
        ],
        out_specs=[vmem] * 2,
        scratch_shapes=[
            pltpu.VMEM((blocks + 1, rows, width), jnp.float32),
            pltpu.VMEM((peers // group, group, depth, width), jnp.bfloat16),
            pltpu.VMEM((blocks, rows, width), jnp.float32),
            pltpu.SemaphoreType.DMA((peers // group,)),
        ],
        out_shape=[jax.ShapeDtypeStruct((blocks // 2, rows, width), jnp.bfloat16)] * 2,
        compiler_params=pltpu.CompilerParams(vmem_limit_bytes=VMEM_SUMS),
        cost_estimate=pl.CostEstimate(
            flops=incoming.size,
            bytes_accessed=2 * incoming.size + 2 * scale.size * width,
            transcendentals=0,
        ),
        name="sums",
    )(labels, incoming, scale)


def back_kernel(*refs, half):
    low, high, (weight, features), out = refs[:4], refs[4:8], refs[8:10], refs[-1]
    group, strips, strip, width = features.shape
    nodes = group * strips * strip

    def run(parts):
        whole = jnp.concatenate([part[...].reshape(nodes, width) for part in parts], axis=1)
        back = lax.dot_general(
            whole, weight[...], (((1,), (0,)), ((), ())), preferred_element_type=jnp.float32
        ).reshape(features.shape)
        mask = features[...].astype(jnp.float32) > 0
        out[...] = jnp.where(mask, back, 0.0).astype(out.dtype)

    @pl.when(pl.program_id(0) < half)
    def _():
        run(low)

    @pl.when(pl.program_id(0) >= half)
    def _():
        run(high)


def back(low, high, weight, features, before, first, rows):
    blocks, strips, strip, width = features.shape
    steps = BACK_STEPS
    group, half, skip = blocks // steps, steps // 2, first // strip
    piece = pl.BlockSpec(
        (pl.Element(group), pl.Element(rows // strip), pl.Element(strip), pl.Element(width)),
        lambda i: (i * group, skip, 0, 0),
    )
    specs = [pl.BlockSpec((group, rows, width), lambda i: (jnp.minimum(i, half - 1), 0, 0))] * 4
    specs += [pl.BlockSpec((group, rows, width), lambda i: (jnp.maximum(i - half, 0), 0, 0))] * 4
    specs += [pl.BlockSpec(weight.shape, lambda i: (0, 0)), piece]
    args = [*low, *high, weight, features]
    aliases = {}
    if before is not None:
        specs.append(pl.BlockSpec(memory_space=pl.ANY))
        args.append(before)
        aliases = {len(args) - 1: 0}
    return pl.pallas_call(
        functools.partial(back_kernel, half=half),
        grid=(steps,),
        in_specs=specs,
        out_specs=piece,
        out_shape=jax.ShapeDtypeStruct(features.shape, jnp.bfloat16),
        input_output_aliases=aliases,
        compiler_params=pltpu.CompilerParams(vmem_limit_bytes=VMEM_BACK),
        cost_estimate=pl.CostEstimate(
            flops=2 * blocks * rows * width * weight.shape[0],
            bytes_accessed=2 * blocks * rows * (weight.shape[0] + 2 * width),
            transcendentals=0,
        ),
        name="back",
    )(*args)


def ring(shift, size):
    return [(i, (i + shift) % size) for i in range(size)]


def exchange(block):
    return lax.all_to_all(block, "row", split_axis=0, concat_axis=0, tiled=True)


def col_near(low, high):
    ahead, behind = ring(1, lax.axis_size("col")), ring(-1, lax.axis_size("col"))
    low_left = lax.ppermute(low, "col", ahead)
    high_right = lax.ppermute(high, "col", behind)
    high_left = lax.ppermute(high, "col", ahead)
    low_right = lax.ppermute(low, "col", behind)
    return low_left, high_left, low_right, high_right


def col_far(low_left, high_right):
    size = lax.axis_size("col")
    return (
        lax.ppermute(low_left, "col", ring(1, size)),
        lax.ppermute(high_right, "col", ring(-1, size)),
    )


def pair_up(own, near, far):
    low = (own[0], near[0], far[0], near[2])
    high = (own[1], near[1], far[1], near[3])
    return low, high


def weight_rows(weight):
    size = lax.axis_size("col")
    width = weight.shape[1]
    me = lax.axis_index("col")
    parts = []
    for shift in range(size):
        start = lax.rem(me + shift, size) * width
        slab = lax.dynamic_slice_in_dim(weight, start, width, 0)
        parts.append(slab if shift == 0 else lax.ppermute(slab, "col", ring(shift, size)))
    return jnp.concatenate(parts, axis=1).T


def per_device(
    grad_out, features, weight, tiles, tile_row_block, tile_owner, tile_local, degrees, live
):
    node_rows, width = grad_out.shape
    size = tiles.shape[1]
    blocks = node_rows // size
    peers = lax.axis_size("row")
    cols = lax.axis_size("col")
    scale = lax.rsqrt(degrees.astype(jnp.float32))
    scaled = (grad_out.astype(jnp.float32) * scale[:, None]).astype(jnp.bfloat16)
    owner = tile_owner[:, 0]
    weight_mine = weight_rows(weight)
    blocked = features.reshape(blocks, size // STRIP, STRIP, width)
    block_scale = scale.reshape(blocks, size)

    starts = [sum(SPLIT[:k]) for k in range(len(SPLIT))]
    gathered = lax.all_gather(features, "col", axis=0).reshape(cols, blocks, size, width)
    outgoing = [
        products(tile_row_block, owner, tile_local, live, tiles, scaled, peers, first, rows, k == 0)
        for k, (first, rows) in enumerate(zip(starts, SPLIT))
    ]
    outgoing[1], weight_mine, gathered = lax.optimization_barrier(
        (outgoing[1], weight_mine, gathered)
    )
    incoming = [exchange(each) for each in outgoing]

    tags = incoming[0][:, PLACES * SPLIT[0], :PLACES].astype(jnp.int32).reshape(-1)
    tags = jnp.where(tags < 0, blocks, tags)
    scales = [block_scale[:, first : first + rows] for first, rows in zip(starts, SPLIT)]

    def local_terms(own, first, rows):
        return lax.dot_general(
            gathered[:, :, first : first + rows],
            jnp.concatenate(own, axis=0),
            (((1, 2), (0, 1)), ((), ())),
            preferred_element_type=jnp.float32,
        )

    own = sums(tags, incoming[0], scales[0], SPLIT[0])
    near = col_near(*own)
    far = col_far(near[0], near[3])
    terms = local_terms(own, 0, SPLIT[0])
    before = back(*pair_up(own, near, far), weight_mine, blocked, None, 0, SPLIT[0])
    incoming[1], terms, _ = lax.optimization_barrier((incoming[1], terms, near))

    own = sums(tags, incoming[1], scales[1], SPLIT[1])
    near = col_near(*own)
    terms = terms + local_terms(own, *SPLIT)
    terms, _ = lax.optimization_barrier((terms, far))
    norm_factor = 1.0 / math.sqrt(node_rows * peers)
    share = cols * width // peers
    pieces = exchange(terms.reshape(peers, share, width).astype(jnp.bfloat16))
    total = jnp.sum(pieces.astype(jnp.float32), axis=0) * norm_factor
    total = jnp.broadcast_to(total.astype(jnp.bfloat16)[None], (peers, share, width))
    near, _ = lax.optimization_barrier((near, total))
    far = col_far(near[0], near[3])
    grad_pre = back(*pair_up(own, near, far), weight_mine, blocked, before, *SPLIT)
    grad_weight = exchange(total).astype(jnp.float32)
    return (grad_pre.reshape(node_rows, width), grad_weight.reshape(cols * width, width))


def solution(mesh):
    return jax.shard_map(
        per_device,
        mesh=mesh,
        in_specs=(
            P("row", "col"),
            P("row", "col"),
            P(None, "col"),
            P("row", None, None),
            P("row"),
            P("row", None),
            P("row"),
            P("row"),
            P("row"),
        ),
        out_specs=(P("row", "col"), P(None, "col")),
        check_vma=False,
    )
```
